32 devices in a mesh: runner: 4 (over z), tile: 8 (over y, x, core).
Axes of the slice: x: 2, y: 2, z: 4, core: 2. Of those that a mesh axis runs over, the one named last changes fastest.
Arguments:
- prior_mean_fields: float32 [3, 64, 512], P(None, 'tile'), may hold values from -0.2 to 0.2
- ensemble_deviations: float32 [128, 3, 64, 512], P('runner', None, 'tile'), may hold values from -0.75 to 0.75
- obs_cell: int32 [8, 4, 256], P('tile', 'runner'), may hold values from 0 to 3071
- obs_value: float32 [8, 4, 256], P('tile', 'runner'), may hold values from -3 to 3
- obs_var: float32 [8, 4, 256], P('tile', 'runner'), may hold values from 0.02 to 0.2
Outputs:
- advanced: float32 [128, 3, 64, 512], P('runner', None, 'tile')
The draws below stay inside these ranges and needn't reach their ends.
Inputs may be any that keep to these rules, and one draw needn't show every extreme that they name: obs_cell[t, s, o] numbers a value of slab (t, s) as field * 2 * 512 + row within the slab * 512 + column.
All inputs are finite; a program needn't handle non-finite values.
Results may differ from the reference program's by a relative error of at most 0.0001.
Values sent between devices are 32-bit elements; how exact they have to be, the bound alone decides.
A program may use at most 128 MiB of HBM per device.

```python
import math
import jax
import jax.numpy as jnp
from jax import lax

RUNNER_ENSEMBLE = 32
MESH_WIDTH_CELLS = 512
OBS = 256
DB_ITERS = 3
ENSEMBLE_SIZE = 128
MESH_LATITUDES = 64
BAND_LATITUDES = 2
N_RUNNER = 4
N_TILE = 8


def plant(entries, own_key, smallest, high):
    index_at = [jax.random.randint(jax.random.fold_in(own_key, axis), (), 0, length) for axis, length in enumerate(entries.shape)]
    widest = entries.shape.index(max(entries.shape))
    neighbour = index_at[:widest] + [(index_at[widest] + 1) % entries.shape[widest]] + index_at[widest + 1:]
    return entries.at[tuple(index_at)].set(smallest).at[tuple(neighbour)].set(high)


def levels(rng, dims, split, least, top_value):
    level = 1.0
    for axis_at, parts in split:
        draws = jax.random.uniform(jax.random.fold_in(jax.random.fold_in(rng, 6), axis_at), (parts,), jnp.float32, least / len(split), top_value / len(split))
        level = level * jnp.repeat(jnp.exp(draws), dims[axis_at] // parts).reshape((-1,) + (1,) * (len(dims) - 1 - axis_at))
    return level


def normal_values(rng, shape, spread, bound, shards=(), held_as=jnp.bfloat16):
    factor_of = levels(rng, shape, shards, -0.22, 0.18) if shards else 1.0
    result = jax.random.normal(rng, shape, jnp.float32) * spread * factor_of
    return jnp.minimum(jnp.maximum(result, -bound), bound).astype(held_as)


def setup_inputs(seed: int = 0) -> dict:
    key_of = jax.random.split(jax.random.key(seed), 6)
    return {
        "prior_mean_fields": jnp.clip(jax.random.uniform(key_of[0], (3, MESH_LATITUDES, MESH_WIDTH_CELLS), jnp.float32, -0.2, 0.2) * levels(key_of[0], (3, MESH_LATITUDES, MESH_WIDTH_CELLS), ((1, 8),), -0.4, 0.0), -0.2, 0.2),
        "ensemble_deviations": normal_values(key_of[1], (ENSEMBLE_SIZE, 3, MESH_LATITUDES, MESH_WIDTH_CELLS), 0.05, 0.75, ((0, 4), (2, 8)), jnp.float32),
        "obs_cell": plant(jax.random.randint(key_of[2], (N_TILE, N_RUNNER, OBS), 0, 3 * BAND_LATITUDES * MESH_WIDTH_CELLS), jax.random.fold_in(key_of[2], 1), 0, (3 * BAND_LATITUDES * MESH_WIDTH_CELLS) - 1).astype(jnp.int32),
        "obs_value": normal_values(key_of[3], (N_TILE, N_RUNNER, OBS), 0.2, 3.0, ((0, 8), (1, 4)), jnp.float32),
        "obs_var": jnp.clip(jnp.exp(math.log(0.2) - 2.3025851 * jax.random.uniform(key_of[4], (N_TILE, N_RUNNER, OBS), jnp.float32) ** levels(key_of[4], (N_TILE, N_RUNNER, OBS), ((0, 8), (1, 4)), -0.2, 0.2)), 0.02, 0.2),
    }


TIME_STEP = 0.25
CORIOLIS = 0.2

def along_x(field):
    return (8.0 * (jnp.roll(field, -1, -1) - jnp.roll(field, 1, -1)) - (jnp.roll(field, -2, -1) - jnp.roll(field, 2, -1))) / 12.0

def along_y(padded):
    return (8.0 * (padded[:, 3:-1] - padded[:, 1:-3]) - (padded[:, 4:] - padded[:, :-4])) / 12.0

def tendency_padded(padded):
    height = padded[:, 0]
    east_speed = padded[:, 1]
    north_speed = padded[:, 2]
    column_depth = 1.0 + height
    flux_x = column_depth * east_speed
    flux_y = column_depth * north_speed
    east_mid = east_speed[:, 2:-2]
    north_mid = north_speed[:, 2:-2]
    height_rate = -(along_x(flux_x[:, 2:-2]) + along_y(flux_y))
    east_rate = -(east_mid * along_x(east_mid) + north_mid * along_y(east_speed)) + CORIOLIS * north_mid - along_x(height[:, 2:-2])
    north_rate = -(east_mid * along_x(north_mid) + north_mid * along_y(north_speed)) - CORIOLIS * east_mid - along_y(height)
    return jnp.stack([height_rate, east_rate, north_rate], axis=1)

def runge_kutta_update(state_now, tendency_of):
    slope_one = tendency_of(state_now)
    slope_two = tendency_of(state_now + 0.5 * TIME_STEP * slope_one)
    slope_three = tendency_of(state_now + 0.5 * TIME_STEP * slope_two)
    slope_four = tendency_of(state_now + TIME_STEP * slope_three)
    return state_now + TIME_STEP / 6.0 * (slope_one + 2.0 * slope_two + 2.0 * slope_three + slope_four)

def wrapped_rate_change(state_now):
    padded = jnp.concatenate([state_now[:, :, -2:], state_now, state_now[:, :, :2]], axis=2)
    return tendency_padded(padded)

def symmetric_inverse(matrix, identity):
    sym = 0.5 * (matrix + matrix.T)
    return jax.scipy.linalg.cho_solve((jnp.linalg.cholesky(sym), True), identity)

def inverse_root(matrix, iterations):
    identity = jnp.eye(matrix.shape[0], dtype=matrix.dtype)
    square_root = matrix
    inverse_part = identity
    for _ in range(iterations):
        inv_square = symmetric_inverse(square_root, identity)
        inv_inverse = symmetric_inverse(inverse_part, identity)
        square_root, inverse_part = (0.5 * (square_root + inv_inverse), 0.5 * (inverse_part + inv_square))
    return inverse_part

def make_transform(gram_matrix, innovation, ensemble):
    identity = jnp.eye(ensemble, dtype=gram_matrix.dtype)
    matrix = identity + gram_matrix / (ensemble - 1.0)
    root = inverse_root(matrix, DB_ITERS)
    inner = jnp.dot(root, innovation, precision=lax.Precision.HIGHEST)
    weights = jnp.dot(root, inner, precision=lax.Precision.HIGHEST) / (ensemble - 1.0)
    return root + weights[:, None]

def correct_with_observations(flat_state, columns):
    member_mean = jnp.mean(flat_state, axis=0)
    return member_mean + jnp.einsum('kc,km->mc', flat_state - member_mean, columns, precision=lax.Precision.HIGHEST)

def reference(prior_mean_fields, ensemble_deviations, obs_cell, obs_value, obs_var):
    ensemble_subsets = ensemble_deviations.reshape(N_RUNNER, RUNNER_ENSEMBLE, 3, MESH_LATITUDES, MESH_WIDTH_CELLS)
    integrate_ensemble_trajectory = lax.map(lambda runner_ensemble_subset: runge_kutta_update(prior_mean_fields[None] + runner_ensemble_subset, wrapped_rate_change), ensemble_subsets)
    integrate_ensemble_trajectory = integrate_ensemble_trajectory.reshape(ENSEMBLE_SIZE, 3, MESH_LATITUDES, MESH_WIDTH_CELLS)
    band_with_margins = integrate_ensemble_trajectory.reshape(ENSEMBLE_SIZE, 3, N_TILE, N_RUNNER, BAND_LATITUDES, MESH_WIDTH_CELLS).transpose(2, 3, 0, 1, 4, 5)
    band_with_margins = band_with_margins.reshape(N_TILE, N_RUNNER, ENSEMBLE_SIZE, 3 * BAND_LATITUDES * MESH_WIDTH_CELLS)
    picked = jnp.take_along_axis(band_with_margins, jnp.broadcast_to(obs_cell[:, :, None, :], (N_TILE, N_RUNNER, ENSEMBLE_SIZE, OBS)), axis=3)
    mean_obs = jnp.mean(picked, axis=2)
    anomaly = picked - mean_obs[:, :, None, :]
    scaled = anomaly / obs_var[:, :, None, :]
    gram_matrix = jnp.einsum('tsko,tslo->kl', scaled, anomaly, precision=lax.Precision.HIGHEST)
    innovation = jnp.einsum('tsko,tso->k', scaled, obs_value - mean_obs, precision=lax.Precision.HIGHEST)
    ensemble_mixing_matrix = make_transform(gram_matrix, innovation, ENSEMBLE_SIZE)
    updated_posterior_fields = correct_with_observations(integrate_ensemble_trajectory.reshape(ENSEMBLE_SIZE, -1), ensemble_mixing_matrix).reshape(N_RUNNER, RUNNER_ENSEMBLE, 3, MESH_LATITUDES, MESH_WIDTH_CELLS)
    advanced = lax.map(lambda runner_ensemble_subset: runner_ensemble_subset + TIME_STEP * wrapped_rate_change(runner_ensemble_subset), updated_posterior_fields)
    return advanced.reshape(ENSEMBLE_SIZE, 3, MESH_LATITUDES, MESH_WIDTH_CELLS)
```

```python
import functools

import jax
import jax.numpy as jnp
import numpy as np
from jax import lax
from jax.experimental import pallas as pl
from jax.experimental.pallas import tpu as pltpu
from jax.sharding import PartitionSpec as P

TIME_STEP = 0.25
CORIOLIS = 0.2
MESH_ID = pl.DeviceIdType.MESH
HIGH = lax.Precision.HIGHEST


def root_terms():
    shifts = [0.0, 1.0, 3.0 - 2.0 * np.sqrt(2.0), 3.0 + 2.0 * np.sqrt(2.0)]
    weights = []
    for shift in shifts:
        at = -shift
        top = at**4 + 28 * at**3 + 70 * at**2 + 28 * at + 1
        bottom = 8.0
        for other in shifts:
            if other != shift:
                bottom *= at + other
        weights.append(top / bottom)
    return [float(s) for s in shifts], [float(w) for w in weights]


def along_x(field):
    width = field.shape[-1]
    axis = field.ndim - 1
    near = pltpu.roll(field, width - 1, axis) - pltpu.roll(field, 1, axis)
    far = pltpu.roll(field, width - 2, axis) - pltpu.roll(field, 2, axis)
    return near * (8.0 / 12.0) - far * (1.0 / 12.0)


def along_y(rows):
    return (rows[3] - rows[1]) * (8.0 / 12.0) - (rows[4] - rows[0]) * (1.0 / 12.0)


def tendency_row(load):
    e = [load(d, 0) for d in range(-2, 3)]
    u = [load(d, 1) for d in range(-2, 3)]
    v = [load(d, 2) for d in range(-2, 3)]
    flux_y = [(1.0 + e[d]) * v[d] if d != 2 else None for d in range(5)]
    flux_x = (1.0 + e[2]) * u[2]
    rate_e = -(along_x(flux_x) + along_y(flux_y))
    rate_u = -(u[2] * along_x(u[2]) + v[2] * along_y(u)) + CORIOLIS * v[2] - along_x(e[2])
    rate_v = -(u[2] * along_x(v[2]) + v[2] * along_y(v)) - CORIOLIS * u[2] - along_y(e)
    return rate_e, rate_u, rate_v


def kernel(
    R, T,
    x0, cell, val, var, out,
    pad, own, slab, cells, picks, picked, parts, part_in, run_in, gram_all, inv, mixed, back,
    halo_s, halo_r, cell_s, cell_r, pick_s, pick_r, g1_s, g1_r, g2_s, g2_r, g3_s, g3_r,
    slab_s, slab_r, back_s, back_r, last_s, last_r,
):
    r = lax.axis_index("runner")
    t = lax.axis_index("tile")
    chunks, rows, fields, mch, C = x0.shape
    M = chunks * mch
    E = M * R
    S = rows // R
    obs = cell.shape[-1]
    h = E // T
    up = lax.rem(t + 1, T)
    down = lax.rem(t + T - 1, T)

    def peer(axis, k):
        return lax.rem((r if axis == "runner" else t) + k, R if axis == "runner" else T)

    def copy(src, dst, send, recv, axis, to):
        return pltpu.make_async_remote_copy(
            src_ref=src, dst_ref=dst, send_sem=send, recv_sem=recv,
            device_id={axis: to}, device_id_type=MESH_ID,
        )

    barrier = pltpu.get_barrier_semaphore()
    for k in range(1, R):
        pl.semaphore_signal(barrier, inc=1, device_id={"runner": peer("runner", k)}, device_id_type=MESH_ID)
    for k in range(1, T):
        pl.semaphore_signal(barrier, inc=1, device_id={"tile": peer("tile", k)}, device_id_type=MESH_ID)
    pl.semaphore_wait(barrier, R - 1 + T - 1)

    cell_copies = [
        copy(cell, cells.at[r], cell_s.at[k - 1], cell_r.at[k - 1], "runner", peer("runner", k))
        for k in range(1, R)
    ]

    def halos(s, c):
        return (
            copy(pad.at[s, c, pl.ds(2, 2)], pad.at[s, c, pl.ds(rows + 2, 2)],
                 halo_s.at[s, 0, c], halo_r.at[s, 0, c], "tile", down),
            copy(pad.at[s, c, pl.ds(rows, 2)], pad.at[s, c, pl.ds(0, 2)],
                 halo_s.at[s, 1, c], halo_r.at[s, 1, c], "tile", up),
        )

    def begin(c, _):
        pad[0, c, pl.ds(2, rows)] = x0[c]
        for one in halos(0, c):
            one.start()
        return 0

    lax.fori_loop(0, chunks, begin, 0)
    for one in cell_copies:
        one.start()
    cells[r] = cell[...]

    for s in range(4):
        weight = TIME_STEP / 6.0 * (1.0 if s in (0, 3) else 2.0)
        ahead = TIME_STEP * (1.0 if s == 2 else 0.5)

        def stage(c, _, s=s, weight=weight, ahead=ahead):
            for one in halos(s, c):
                one.wait_recv()

            def one_row(j, _):
                rates = tendency_row(lambda d, f: pad[s, c, j + 2 + d, f])
                for f, rate in enumerate(rates):
                    if s == 0:
                        own[c, j, f] = x0[c, j, f] + weight * rate
                    else:
                        own[c, j, f] = own[c, j, f] + weight * rate
                    if s < 3:
                        pad[s + 1, c, j + 2, f] = x0[c, j, f] + ahead * rate
                return 0

            lax.fori_loop(0, rows, one_row, 0)
            if s < 3:
                for one in halos(s + 1, c):
                    one.start()
            return 0

        lax.fori_loop(0, chunks, stage, 0)

    for one in cell_copies:
        one.wait_recv()
    column = lax.broadcasted_iota(jnp.int32, (C, obs), 0)

    def pick(q, _):
        numbers = cells[q]
        total = jnp.zeros((3 * M, obs), jnp.float32)
        for j in range(S):
            for f in range(fields):
                value = own[:, q * S + j, f].reshape(M, C)
                first = value.astype(jnp.bfloat16)
                rest = value - first.astype(jnp.float32)
                second = rest.astype(jnp.bfloat16)
                third = (rest - second.astype(jnp.float32)).astype(jnp.bfloat16)
                hot = jnp.where(column == numbers - (f * S + j) * C, 1.0, 0.0).astype(jnp.bfloat16)
                total = total + jnp.dot(
                    jnp.concatenate([first, second, third], axis=0), hot,
                    preferred_element_type=jnp.float32,
                )
        picks[q] = total[:M] + total[M : 2 * M] + total[2 * M :]
        return 0

    lax.fori_loop(0, R, pick, 0)
    pick_copies = [
        copy(picks.at[peer("runner", k)], picked.at[r], pick_s.at[k - 1], pick_r.at[k - 1],
             "runner", peer("runner", k))
        for k in range(1, R)
    ]
    for one in pick_copies:
        one.start()
    picked[r] = picks[r]
    for one in pick_copies:
        one.wait_recv()

    seen = picked[...].reshape(E, obs)
    mean = jnp.sum(seen, axis=0, keepdims=True) * (1.0 / E)
    anomaly = seen - mean
    scaled = anomaly / var[...]
    gram = lax.dot_general(
        scaled, anomaly, (((1,), (1,)), ((), ())), precision=HIGH, preferred_element_type=jnp.float32
    )
    innovation = jnp.sum(scaled * (val[...] - mean), axis=1, keepdims=True)
    parts[:, :, :E] = gram.reshape(T, h, E)
    parts[:, :, E:] = jnp.broadcast_to(innovation, (E, 128)).reshape(T, h, 128)

    first_copies = [
        copy(parts.at[peer("tile", k)], part_in.at[t], g1_s.at[k - 1], g1_r.at[k - 1], "tile", peer("tile", k))
        for k in range(1, T)
    ]
    for one in first_copies:
        one.start()
    part_in[t] = parts[t]
    for one in first_copies:
        one.wait_recv()
    run_in[r] = jnp.sum(part_in[...], axis=0)
    second_copies = [
        copy(run_in.at[r], run_in.at[r], g2_s.at[k - 1], g2_r.at[k - 1], "runner", peer("runner", k))
        for k in range(1, R)
    ]
    for one in second_copies:
        one.start()
    for one in second_copies:
        one.wait_recv()
    gram_all[t] = jnp.sum(run_in[...], axis=0)
    third_copies = [
        copy(gram_all.at[t], gram_all.at[t], g3_s.at[k - 1], g3_r.at[k - 1], "tile", peer("tile", k))
        for k in range(1, T)
    ]
    for one in third_copies:
        one.start()

    slab_copies = [
        copy(own.at[:, pl.ds(peer("runner", k) * S, S)], slab.at[r], slab_s.at[k - 1], slab_r.at[k - 1],
             "runner", peer("runner", k))
        for k in range(1, R)
    ]
    for one in slab_copies:
        one.start()
    slab[r] = own[:, pl.ds(r * S, S)]
    for one in third_copies:
        one.wait_recv()

    total = gram_all[...].reshape(E, E + 128)
    eye = jnp.where(
        lax.broadcasted_iota(jnp.int32, (E, E), 0) == lax.broadcasted_iota(jnp.int32, (E, E), 1), 1.0, 0.0
    )
    shifts, weights = root_terms()
    for i, shift in enumerate(shifts):
        inv[i] = total[:, :E] * (1.0 / (E - 1.0)) + (1.0 + shift) * eye
    lane = lax.broadcasted_iota(jnp.int32, (1, E), 1)

    def sweep(k, _):
        here = lane == k
        for i in range(len(shifts)):
            now = inv[i]
            row = inv[i, pl.ds(k, 1), :]
            col = jnp.sum(jnp.where(here, now, 0.0), axis=1, keepdims=True)
            pivot = 1.0 / jnp.sum(jnp.where(here, row, 0.0), axis=1, keepdims=True)
            row = jnp.where(here, -pivot, row * pivot)
            inv[i] = jnp.where(here, 0.0, now) - col * row
            inv[i, pl.ds(k, 1), :] = row
        return 0

    lax.fori_loop(0, E, sweep, 0)
    root = 0.125 * eye
    for i, weight in enumerate(weights):
        root = root - weight * inv[i]
    inner = jnp.dot(root, total[:, E:], precision=HIGH, preferred_element_type=jnp.float32)
    extra = jnp.dot(root, inner, precision=HIGH, preferred_element_type=jnp.float32) * (1.0 / (E - 1.0))
    transform = root + extra[:, :1]
    transform = transform - jnp.sum(transform, axis=0, keepdims=True) * (1.0 / E) + 1.0 / E
    turned = transform.T

    for one in slab_copies:
        one.wait_recv()
    back_copies = [
        copy(mixed.at[peer("runner", k)], back.at[pl.ds(2 + r * S, S)], back_s.at[k - 1], back_r.at[k - 1],
             "runner", peer("runner", k))
        for k in range(1, R)
    ]
    for j in range(S):
        for f in range(fields):
            value = slab[:, :, j, f].reshape(E, C)
            result = jnp.dot(turned, value, precision=HIGH, preferred_element_type=jnp.float32)
            mixed[:, j, f] = result.reshape(R, M, C)
    for one in back_copies:
        one.start()
    back[pl.ds(2 + r * S, S)] = mixed[r]
    for one in back_copies:
        one.wait_recv()

    last_copies = [
        copy(back.at[pl.ds(2, 2)], back.at[pl.ds(rows + 2, 2)], last_s.at[0], last_r.at[0], "tile", down),
        copy(back.at[pl.ds(rows, 2)], back.at[pl.ds(0, 2)], last_s.at[1], last_r.at[1], "tile", up),
    ]
    for one in last_copies:
        one.start()
    for one in last_copies:
        one.wait_recv()

    def last_row(n, _):
        j = n // chunks
        members = pl.ds(pl.multiple_of((n % chunks) * mch, mch), mch)
        rates = tendency_row(lambda d, f: back[j + 2 + d, f, members, :])
        for f, rate in enumerate(rates):
            out[j, f, members, :] = back[j + 2, f, members, :] + TIME_STEP * rate
        return 0

    lax.fori_loop(0, rows * chunks, last_row, 0)

    def drain(c, _):
        for s in range(4):
            for one in halos(s, c):
                one.wait_send()
        return 0

    lax.fori_loop(0, chunks, drain, 0)
    for group in (cell_copies, pick_copies, first_copies, second_copies, third_copies,
                  slab_copies, back_copies, last_copies):
        for one in group:
            one.wait_send()


def per_device(R, T, prior_mean_fields, ensemble_deviations, obs_cell, obs_value, obs_var):
    M, fields, rows, C = ensemble_deviations.shape
    E = M * R
    S = rows // R
    mch = 8
    chunks = M // mch
    obs = obs_cell.shape[-1]
    h = E // T
    start = prior_mean_fields[None] + ensemble_deviations
    start = start.reshape(chunks, mch, fields, rows, C).transpose(0, 3, 2, 1, 4)
    f32 = jnp.float32
    dma = pltpu.SemaphoreType.DMA
    vmem = pl.BlockSpec(memory_space=pltpu.VMEM)
    pairs = lambda n: [dma((n,)), dma((n,))]
    result = pl.pallas_call(
        functools.partial(kernel, R, T),
        out_shape=jax.ShapeDtypeStruct((rows, fields, M, C), f32),
        in_specs=[vmem] * 4,
        out_specs=vmem,
        scratch_shapes=[
            pltpu.VMEM((4, chunks, rows + 4, fields, mch, C), f32),
            pltpu.VMEM((chunks, rows, fields, mch, C), f32),
            pltpu.VMEM((R, chunks, S, fields, mch, C), f32),
            pltpu.VMEM((R, 1, obs), jnp.int32),
            pltpu.VMEM((R, M, obs), f32),
            pltpu.VMEM((R, M, obs), f32),
            pltpu.VMEM((T, h, E + 128), f32),
            pltpu.VMEM((T, h, E + 128), f32),
            pltpu.VMEM((R, h, E + 128), f32),
            pltpu.VMEM((T, h, E + 128), f32),
            pltpu.VMEM((4, E, E), f32),
            pltpu.VMEM((R, S, fields, M, C), f32),
            pltpu.VMEM((rows + 4, fields, M, C), f32),
            dma((4, 2, chunks)), dma((4, 2, chunks)),
            *pairs(R - 1), *pairs(R - 1), *pairs(T - 1), *pairs(R - 1), *pairs(T - 1),
            *pairs(R - 1), *pairs(R - 1), *pairs(2),
        ],
        compiler_params=pltpu.CompilerParams(
            collective_id=0, has_side_effects=True, vmem_limit_bytes=48 * 1024 * 1024
        ),
        name="forecast",
    )(start, obs_cell[0], obs_value[0], obs_var[0])
    return result.transpose(2, 1, 0, 3)


def solution(mesh):
    placed = (
        P(None, "tile", None),
        P("runner", None, "tile", None),
        P("tile", "runner", None),
        P("tile", "runner", None),
        P("tile", "runner", None),
    )
    return jax.shard_map(
        functools.partial(per_device, mesh.shape["runner"], mesh.shape["tile"]),
        mesh=mesh,
        in_specs=placed,
        out_specs=P("runner", None, "tile", None),
        check_vma=False,
    )
```

```python
import functools

import jax
import jax.numpy as jnp
import numpy as np
from jax import lax
from jax.experimental import pallas as pl
from jax.experimental.pallas import tpu as pltpu
from jax.sharding import PartitionSpec as P

TIME_STEP = 0.25
CORIOLIS = 0.2
MESH_ID = pl.DeviceIdType.MESH
HIGH = lax.Precision.HIGHEST


def root_terms():
    shifts = [0.0, 1.0, 3.0 - 2.0 * np.sqrt(2.0), 3.0 + 2.0 * np.sqrt(2.0)]
    weights = []
    for shift in shifts:
        at = -shift
        top = at**4 + 28 * at**3 + 70 * at**2 + 28 * at + 1
        bottom = 8.0
        for other in shifts:
            if other != shift:
                bottom *= at + other
        weights.append(top / bottom)
    return [float(s) for s in shifts], [float(w) for w in weights]


def along_x(field):
    width = field.shape[-1]
    axis = field.ndim - 1
    near = pltpu.roll(field, width - 1, axis) - pltpu.roll(field, 1, axis)
    far = pltpu.roll(field, width - 2, axis) - pltpu.roll(field, 2, axis)
    return near * (8.0 / 12.0) - far * (1.0 / 12.0)


def along_y(rows):
    return (rows[3] - rows[1]) * (8.0 / 12.0) - (rows[4] - rows[0]) * (1.0 / 12.0)


def tendency_row(load):
    e = [load(d, 0) for d in range(-2, 3)]
    u = [load(d, 1) for d in range(-2, 3)]
    v = [load(d, 2) for d in range(-2, 3)]
    flux_y = [(1.0 + e[d]) * v[d] if d != 2 else None for d in range(5)]
    flux_x = (1.0 + e[2]) * u[2]
    rate_e = -(along_x(flux_x) + along_y(flux_y))
    rate_u = -(u[2] * along_x(u[2]) + v[2] * along_y(u)) + CORIOLIS * v[2] - along_x(e[2])
    rate_v = -(u[2] * along_x(v[2]) + v[2] * along_y(v)) - CORIOLIS * u[2] - along_y(e)
    return rate_e, rate_u, rate_v


def kernel(
    R, T,
    x0, cell, val, var, out,
    pad, own, slab, cells, picks, picked, parts, part_in, run_in, gram_all, inv, mixed, back,
    halo_s, halo_r, cell_s, cell_r, pick_s, pick_r, g1_s, g1_r, g2_s, g2_r, g3_s, g3_r,
    slab_s, slab_r, back_s, back_r, last_s, last_r,
):
    r = lax.axis_index("runner")
    t = lax.axis_index("tile")
    chunks, rows, fields, mch, C = x0.shape
    M = chunks * mch
    E = M * R
    S = rows // R
    obs = cell.shape[-1]
    h = E // T
    up = lax.rem(t + 1, T)
    down = lax.rem(t + T - 1, T)

    def peer(axis, k):
        return lax.rem((r if axis == "runner" else t) + k, R if axis == "runner" else T)

    def copy(src, dst, send, recv, axis, to):
        return pltpu.make_async_remote_copy(
            src_ref=src, dst_ref=dst, send_sem=send, recv_sem=recv,
            device_id={axis: to}, device_id_type=MESH_ID,
        )

    barrier = pltpu.get_barrier_semaphore()
    for k in range(1, R):
        pl.semaphore_signal(barrier, inc=1, device_id={"runner": peer("runner", k)}, device_id_type=MESH_ID)
    for k in range(1, T):
        pl.semaphore_signal(barrier, inc=1, device_id={"tile": peer("tile", k)}, device_id_type=MESH_ID)
    pl.semaphore_wait(barrier, R - 1 + T - 1)

    cell_copies = [
        copy(cell, cells.at[r], cell_s.at[k - 1], cell_r.at[k - 1], "runner", peer("runner", k))
        for k in range(1, R)
    ]

    def halos(s, c):
        return (
            copy(pad.at[s, c, pl.ds(2, 2)], pad.at[s, c, pl.ds(rows + 2, 2)],
                 halo_s.at[s, 0, c], halo_r.at[s, 0, c], "tile", down),
            copy(pad.at[s, c, pl.ds(rows, 2)], pad.at[s, c, pl.ds(0, 2)],
                 halo_s.at[s, 1, c], halo_r.at[s, 1, c], "tile", up),
        )

    def slab_copies(c):
        return [
            copy(own.at[c, pl.ds(peer("runner", k) * S, S)], slab.at[r, c], slab_s.at[k - 1, c],
                 slab_r.at[k - 1, c], "runner", peer("runner", k))
            for k in range(1, R)
        ]

    def start_slabs(c, _):
        for one in slab_copies(c):
            one.start()
        return 0

    def wait_slabs(c, _):
        for one in slab_copies(c):
            one.wait_recv()
        return 0

    def begin(c, _):
        pad[0, c, pl.ds(2, rows)] = x0[c]
        for one in halos(0, c):
            one.start()
        return 0

    lax.fori_loop(0, chunks, begin, 0)
    for one in cell_copies:
        one.start()
    cells[r] = cell[...]

    for s in range(4):
        weight = TIME_STEP / 6.0 * (1.0 if s in (0, 3) else 2.0)
        ahead = TIME_STEP * (1.0 if s == 2 else 0.5)

        def stage(c, _, s=s, weight=weight, ahead=ahead):
            for one in halos(s, c):
                one.wait_recv()

            def one_row(j, _):
                rates = tendency_row(lambda d, f: pad[s, c, j + 2 + d, f])
                for f, rate in enumerate(rates):
                    if s == 0:
                        own[c, j, f] = x0[c, j, f] + weight * rate
                    else:
                        own[c, j, f] = own[c, j, f] + weight * rate
                    if s < 3:
                        pad[s + 1, c, j + 2, f] = x0[c, j, f] + ahead * rate
                return 0

            lax.fori_loop(0, rows, one_row, 0)
            if s < 3:
                for one in halos(s + 1, c):
                    one.start()
            else:
                slab[r, c] = own[c, pl.ds(r * S, S)]
            return 0

        lax.fori_loop(0, chunks, stage, 0)

    for one in cell_copies:
        one.wait_recv()
    column = lax.broadcasted_iota(jnp.int32, (C, obs), 0)

    def pick(q, _):
        numbers = cells[q]
        total = jnp.zeros((3 * M, obs), jnp.float32)
        for j in range(S):
            for f in range(fields):
                value = own[:, q * S + j, f].reshape(M, C)
                first = value.astype(jnp.bfloat16)
                rest = value - first.astype(jnp.float32)
                second = rest.astype(jnp.bfloat16)
                third = (rest - second.astype(jnp.float32)).astype(jnp.bfloat16)
                hot = jnp.where(column == numbers - (f * S + j) * C, 1.0, 0.0).astype(jnp.bfloat16)
                total = total + jnp.dot(
                    jnp.concatenate([first, second, third], axis=0), hot,
                    preferred_element_type=jnp.float32,
                )
        picks[q] = total[:M] + total[M : 2 * M] + total[2 * M :]
        return 0

    lax.fori_loop(0, R, pick, 0)
    pick_copies = [
        copy(picks.at[peer("runner", k)], picked.at[r], pick_s.at[k - 1], pick_r.at[k - 1],
             "runner", peer("runner", k))
        for k in range(1, R)
    ]
    for one in pick_copies:
        one.start()
    picked[r] = picks[r]
    for one in pick_copies:
        one.wait_recv()

    seen = picked[...].reshape(E, obs)
    mean = jnp.sum(seen, axis=0, keepdims=True) * (1.0 / E)
    anomaly = seen - mean
    scaled = anomaly / var[...]
    gram = lax.dot_general(
        scaled, anomaly, (((1,), (1,)), ((), ())), precision=HIGH, preferred_element_type=jnp.float32
    )
    innovation = jnp.sum(scaled * (val[...] - mean), axis=1, keepdims=True)
    parts[:, :, :E] = gram.reshape(T, h, E)
    parts[:, :, E:] = jnp.broadcast_to(innovation, (E, 128)).reshape(T, h, 128)

    first_copies = [
        copy(parts.at[peer("tile", k)], part_in.at[t], g1_s.at[k - 1], g1_r.at[k - 1], "tile", peer("tile", k))
        for k in range(1, T)
    ]
    for one in first_copies:
        one.start()
    part_in[t] = parts[t]
    for one in first_copies:
        one.wait_recv()
    run_in[r] = jnp.sum(part_in[...], axis=0)
    second_copies = [
        copy(run_in.at[r], run_in.at[r], g2_s.at[k - 1], g2_r.at[k - 1], "runner", peer("runner", k))
        for k in range(1, R)
    ]
    for one in second_copies:
        one.start()
    for one in second_copies:
        one.wait_recv()
    gram_all[t] = jnp.sum(run_in[...], axis=0)
    third_copies = [
        copy(gram_all.at[t], gram_all.at[t], g3_s.at[k - 1], g3_r.at[k - 1], "tile", peer("tile", k))
        for k in range(1, T)
    ]
    for one in third_copies:
        one.start()

    lax.fori_loop(0, chunks, start_slabs, 0)
    for one in third_copies:
        one.wait_recv()

    total = gram_all[...].reshape(E, E + 128)
    eye = jnp.where(
        lax.broadcasted_iota(jnp.int32, (E, E), 0) == lax.broadcasted_iota(jnp.int32, (E, E), 1), 1.0, 0.0
    )
    shifts, weights = root_terms()
    for i, shift in enumerate(shifts):
        inv[i] = total[:, :E] * (1.0 / (E - 1.0)) + (1.0 + shift) * eye
    lane = lax.broadcasted_iota(jnp.int32, (1, E), 1)
    place = lax.broadcasted_iota(jnp.int32, (8, 1), 0)
    count = len(shifts)

    def sweep(n, _):
        at = pl.multiple_of(n * 8, 8)
        before = [inv[i, pl.ds(at, 8), :] for i in range(count)]
        panel = list(before)
        for k in range(8):
            here = lane == at + k
            for i in range(count):
                now = panel[i]
                col = jnp.sum(jnp.where(here, now, 0.0), axis=1, keepdims=True)
                pivot = 1.0 / col[k : k + 1]
                row = jnp.where(here, -pivot, now[k : k + 1] * pivot)
                panel[i] = jnp.where(place == k, row, jnp.where(here, 0.0, now) - col * row)
        inside = (lane >= at) & (lane < at + 8)
        for i in range(count):
            change = lax.dot_general(
                before[i], panel[i], (((0,), (0,)), ((), ())), precision=HIGH,
                preferred_element_type=jnp.float32,
            )
            inv[i] = jnp.where(inside, 0.0, inv[i]) - change
            inv[i, pl.ds(at, 8), :] = panel[i]
        return 0

    lax.fori_loop(0, E // 8, sweep, 0)
    root = 0.125 * eye
    for i, weight in enumerate(weights):
        root = root - weight * inv[i]
    inner = jnp.dot(root, total[:, E:], precision=HIGH, preferred_element_type=jnp.float32)
    extra = jnp.dot(root, inner, precision=HIGH, preferred_element_type=jnp.float32) * (1.0 / (E - 1.0))
    transform = root + extra[:, :1]
    transform = transform - jnp.sum(transform, axis=0, keepdims=True) * (1.0 / E) + 1.0 / E
    turned = transform.T

    lax.fori_loop(0, chunks, wait_slabs, 0)

    def back_copies(c):
        return [
            copy(mixed.at[peer("runner", k), c], back.at[c, pl.ds(2 + r * S, S)], back_s.at[k - 1, c],
                 back_r.at[k - 1, c], "runner", peer("runner", k))
            for k in range(1, R)
        ]

    for j in range(S):
        for f in range(fields):
            value = slab[:, :, j, f].reshape(E, C)
            result = jnp.dot(turned, value, precision=HIGH, preferred_element_type=jnp.float32)
            mixed[:, :, j, f] = result.reshape(R, chunks, mch, C)

    def give_back(c, _):
        for one in back_copies(c):
            one.start()
        back[c, pl.ds(2 + r * S, S)] = mixed[r, c]
        return 0

    lax.fori_loop(0, chunks, give_back, 0)

    def last_copies(c):
        return (
            copy(back.at[c, pl.ds(2, 2)], back.at[c, pl.ds(rows + 2, 2)], last_s.at[0, c], last_r.at[0, c],
                 "tile", down),
            copy(back.at[c, pl.ds(rows, 2)], back.at[c, pl.ds(0, 2)], last_s.at[1, c], last_r.at[1, c],
                 "tile", up),
        )

    def last_begin(c, _):
        for one in back_copies(c):
            one.wait_recv()
        for one in last_copies(c):
            one.start()
        return 0

    def last_end(c, _):
        for one in last_copies(c):
            one.wait_recv()

        def last_row(j, _):
            rates = tendency_row(lambda d, f: back[c, j + 2 + d, f])
            for f, rate in enumerate(rates):
                out[c, j, f] = back[c, j + 2, f] + TIME_STEP * rate
            return 0

        lax.fori_loop(0, rows, last_row, 0)
        return 0

    def last_both(c, _):
        last_begin(c, 0)
        last_end(c - 1, 0)
        return 0

    last_begin(0, 0)
    lax.fori_loop(1, chunks, last_both, 0)
    last_end(chunks - 1, 0)

    def drain(c, _):
        for s in range(4):
            for one in halos(s, c):
                one.wait_send()
        for one in (*slab_copies(c), *back_copies(c), *last_copies(c)):
            one.wait_send()
        return 0

    lax.fori_loop(0, chunks, drain, 0)
    for group in (cell_copies, pick_copies, first_copies, second_copies, third_copies):
        for one in group:
            one.wait_send()


def per_device(R, T, prior_mean_fields, ensemble_deviations, obs_cell, obs_value, obs_var):
    M, fields, rows, C = ensemble_deviations.shape
    E = M * R
    S = rows // R
    mch = 8
    chunks = M // mch
    obs = obs_cell.shape[-1]
    h = E // T
    start = prior_mean_fields[None] + ensemble_deviations
    start = start.reshape(chunks, mch, fields, rows, C).transpose(0, 3, 2, 1, 4)
    f32 = jnp.float32
    dma = pltpu.SemaphoreType.DMA
    vmem = pl.BlockSpec(memory_space=pltpu.VMEM)
    pairs = lambda n: [dma((n,)), dma((n,))]
    result = pl.pallas_call(
        functools.partial(kernel, R, T),
        out_shape=jax.ShapeDtypeStruct((chunks, rows, fields, mch, C), f32),
        in_specs=[vmem] * 4,
        out_specs=vmem,
        scratch_shapes=[
            pltpu.VMEM((4, chunks, rows + 4, fields, mch, C), f32),
            pltpu.VMEM((chunks, rows, fields, mch, C), f32),
            pltpu.VMEM((R, chunks, S, fields, mch, C), f32),
            pltpu.VMEM((R, 1, obs), jnp.int32),
            pltpu.VMEM((R, M, obs), f32),
            pltpu.VMEM((R, M, obs), f32),
            pltpu.VMEM((T, h, E + 128), f32),
            pltpu.VMEM((T, h, E + 128), f32),
            pltpu.VMEM((R, h, E + 128), f32),
            pltpu.VMEM((T, h, E + 128), f32),
            pltpu.VMEM((4, E, E), f32),
            pltpu.VMEM((R, chunks, S, fields, mch, C), f32),
            pltpu.VMEM((chunks, rows + 4, fields, mch, C), f32),
            dma((4, 2, chunks)), dma((4, 2, chunks)),
            *pairs(R - 1), *pairs(R - 1), *pairs(T - 1), *pairs(R - 1), *pairs(T - 1),
            dma((R - 1, chunks)), dma((R - 1, chunks)), dma((R - 1, chunks)), dma((R - 1, chunks)),
            dma((2, chunks)), dma((2, chunks)),
        ],
        compiler_params=pltpu.CompilerParams(
            collective_id=0, has_side_effects=True, vmem_limit_bytes=48 * 1024 * 1024
        ),
        name="forecast",
    )(start, obs_cell[0], obs_value[0], obs_var[0])
    return result.transpose(0, 3, 2, 1, 4).reshape(M, fields, rows, C)


def solution(mesh):
    placed = (
        P(None, "tile", None),
        P("runner", None, "tile", None),
        P("tile", "runner", None),
        P("tile", "runner", None),
        P("tile", "runner", None),
    )
    return jax.shard_map(
        functools.partial(per_device, mesh.shape["runner"], mesh.shape["tile"]),
        mesh=mesh,
        in_specs=placed,
        out_specs=P("runner", None, "tile", None),
        check_vma=False,
    )
```

```python
import functools

import jax
import jax.numpy as jnp
import numpy as np
from jax import lax
from jax.experimental import pallas as pl
from jax.experimental.pallas import tpu as pltpu
from jax.sharding import PartitionSpec as P

TIME_STEP = 0.25
CORIOLIS = 0.2
MESH_ID = pl.DeviceIdType.MESH
HIGH = lax.Precision.HIGHEST


def root_terms():
    shifts = [0.0, 1.0, 3.0 - 2.0 * np.sqrt(2.0), 3.0 + 2.0 * np.sqrt(2.0)]
    weights = []
    for shift in shifts:
        at = -shift
        top = at**4 + 28 * at**3 + 70 * at**2 + 28 * at + 1
        bottom = 8.0
        for other in shifts:
            if other != shift:
                bottom *= at + other
        weights.append(top / bottom)
    return [float(s) for s in shifts], [float(w) for w in weights]


def along_x(field):
    width = field.shape[-1]
    axis = field.ndim - 1
    near = pltpu.roll(field, width - 1, axis) - pltpu.roll(field, 1, axis)
    far = pltpu.roll(field, width - 2, axis) - pltpu.roll(field, 2, axis)
    return near * (8.0 / 12.0) - far * (1.0 / 12.0)


def along_y(rows):
    return (rows[3] - rows[1]) * (8.0 / 12.0) - (rows[4] - rows[0]) * (1.0 / 12.0)


def tendency_row(load):
    e = [load(d, 0) for d in range(-2, 3)]
    u = [load(d, 1) for d in range(-2, 3)]
    v = [load(d, 2) for d in range(-2, 3)]
    flux_y = [(1.0 + e[d]) * v[d] if d != 2 else None for d in range(5)]
    flux_x = (1.0 + e[2]) * u[2]
    rate_e = -(along_x(flux_x) + along_y(flux_y))
    rate_u = -(u[2] * along_x(u[2]) + v[2] * along_y(u)) + CORIOLIS * v[2] - along_x(e[2])
    rate_v = -(u[2] * along_x(v[2]) + v[2] * along_y(v)) - CORIOLIS * u[2] - along_y(e)
    return rate_e, rate_u, rate_v


def kernel(
    R, T,
    x0, cell, val, var, out,
    pad, own, slab, cells, picks, picked, parts, part_in, run_in, gram_all, inv, mixed, back,
    halo_s, halo_r, cell_s, cell_r, pick_s, pick_r, g1_s, g1_r, g2_s, g2_r, g3_s, g3_r,
    slab_s, slab_r, back_s, back_r, last_s, last_r,
):
    r = lax.axis_index("runner")
    t = lax.axis_index("tile")
    chunks, rows, fields, mch, C = x0.shape
    M = chunks * mch
    E = M * R
    S = rows // R
    obs = cell.shape[-1]
    h = E // T
    early = min(1, chunks)
    up = lax.rem(t + 1, T)
    down = lax.rem(t + T - 1, T)

    def peer(axis, k):
        return lax.rem((r if axis == "runner" else t) + k, R if axis == "runner" else T)

    def copy(src, dst, send, recv, axis, to):
        return pltpu.make_async_remote_copy(
            src_ref=src, dst_ref=dst, send_sem=send, recv_sem=recv,
            device_id={axis: to}, device_id_type=MESH_ID,
        )

    barrier = pltpu.get_barrier_semaphore()
    for k in range(1, R):
        pl.semaphore_signal(barrier, inc=1, device_id={"runner": peer("runner", k)}, device_id_type=MESH_ID)
    for k in range(1, T):
        pl.semaphore_signal(barrier, inc=1, device_id={"tile": peer("tile", k)}, device_id_type=MESH_ID)
    pl.semaphore_wait(barrier, R - 1 + T - 1)

    cell_copies = [
        copy(cell, cells.at[r], cell_s.at[k - 1], cell_r.at[k - 1], "runner", peer("runner", k))
        for k in range(1, R)
    ]

    def halos(s, c):
        return (
            copy(pad.at[s, c, pl.ds(2, 2)], pad.at[s, c, pl.ds(rows + 2, 2)],
                 halo_s.at[s, 0, c], halo_r.at[s, 0, c], "tile", down),
            copy(pad.at[s, c, pl.ds(rows, 2)], pad.at[s, c, pl.ds(0, 2)],
                 halo_s.at[s, 1, c], halo_r.at[s, 1, c], "tile", up),
        )

    def slab_copies(c):
        return [
            copy(own.at[c, pl.ds(peer("runner", k) * S, S)], slab.at[r, c], slab_s.at[k - 1, c],
                 slab_r.at[k - 1, c], "runner", peer("runner", k))
            for k in range(1, R)
        ]

    def start_slabs(c, _):
        for one in slab_copies(c):
            one.start()
        return 0

    def wait_slabs(c, _):
        for one in slab_copies(c):
            one.wait_recv()
        return 0

    def begin(c, _):
        pad[0, c, pl.ds(2, rows)] = x0[c]
        for one in halos(0, c):
            one.start()
        return 0

    lax.fori_loop(0, chunks, begin, 0)
    for one in cell_copies:
        one.start()
    cells[r] = cell[...]

    for s in range(4):
        weight = TIME_STEP / 6.0 * (1.0 if s in (0, 3) else 2.0)
        ahead = TIME_STEP * (1.0 if s == 2 else 0.5)

        def stage(c, _, s=s, weight=weight, ahead=ahead):
            for one in halos(s, c):
                one.wait_recv()

            def one_row(j, _):
                rates = tendency_row(lambda d, f: pad[s, c, j + 2 + d, f])
                for f, rate in enumerate(rates):
                    if s == 0:
                        own[c, j, f] = x0[c, j, f] + weight * rate
                    else:
                        own[c, j, f] = own[c, j, f] + weight * rate
                    if s < 3:
                        pad[s + 1, c, j + 2, f] = x0[c, j, f] + ahead * rate
                return 0

            lax.fori_loop(0, rows, one_row, 0)
            if s < 3:
                for one in halos(s + 1, c):
                    one.start()
            else:
                slab[r, c] = own[c, pl.ds(r * S, S)]
            return 0

        if s < 3:
            lax.fori_loop(0, chunks, stage, 0)
        else:
            lax.fori_loop(0, early, stage, 0)
            lax.fori_loop(0, early, start_slabs, 0)
            lax.fori_loop(early, chunks, stage, 0)

    for one in cell_copies:
        one.wait_recv()
    column = lax.broadcasted_iota(jnp.int32, (C, obs), 0)

    def pick(q, _):
        numbers = cells[q]
        total = jnp.zeros((3 * M, obs), jnp.float32)
        for j in range(S):
            for f in range(fields):
                value = own[:, q * S + j, f].reshape(M, C)
                first = value.astype(jnp.bfloat16)
                rest = value - first.astype(jnp.float32)
                second = rest.astype(jnp.bfloat16)
                third = (rest - second.astype(jnp.float32)).astype(jnp.bfloat16)
                hot = jnp.where(column == numbers - (f * S + j) * C, 1.0, 0.0).astype(jnp.bfloat16)
                total = total + jnp.dot(
                    jnp.concatenate([first, second, third], axis=0), hot,
                    preferred_element_type=jnp.float32,
                )
        picks[q] = total[:M] + total[M : 2 * M] + total[2 * M :]
        return 0

    lax.fori_loop(0, R, pick, 0)
    pick_copies = [
        copy(picks.at[peer("runner", k)], picked.at[r], pick_s.at[k - 1], pick_r.at[k - 1],
             "runner", peer("runner", k))
        for k in range(1, R)
    ]
    for one in pick_copies:
        one.start()
    picked[r] = picks[r]
    for one in pick_copies:
        one.wait_recv()

    seen = picked[...].reshape(E, obs)
    mean = jnp.sum(seen, axis=0, keepdims=True) * (1.0 / E)
    anomaly = seen - mean
    scaled = anomaly / var[...]
    gram = lax.dot_general(
        scaled, anomaly, (((1,), (1,)), ((), ())), precision=HIGH, preferred_element_type=jnp.float32
    )
    innovation = jnp.sum(scaled * (val[...] - mean), axis=1, keepdims=True)
    parts[:, :, :E] = gram.reshape(T, h, E)
    parts[:, :, E:] = jnp.broadcast_to(innovation, (E, 128)).reshape(T, h, 128)

    first_copies = [
        copy(parts.at[peer("tile", k)], part_in.at[t], g1_s.at[k - 1], g1_r.at[k - 1], "tile", peer("tile", k))
        for k in range(1, T)
    ]
    for one in first_copies:
        one.start()
    part_in[t] = parts[t]
    for one in first_copies:
        one.wait_recv()
    run_in[r] = jnp.sum(part_in[...], axis=0)
    second_copies = [
        copy(run_in.at[r], run_in.at[r], g2_s.at[k - 1], g2_r.at[k - 1], "runner", peer("runner", k))
        for k in range(1, R)
    ]
    for one in second_copies:
        one.start()
    for one in second_copies:
        one.wait_recv()
    gram_all[t] = jnp.sum(run_in[...], axis=0)
    third_copies = [
        copy(gram_all.at[t], gram_all.at[t], g3_s.at[k - 1], g3_r.at[k - 1], "tile", peer("tile", k))
        for k in range(1, T)
    ]
    for one in third_copies:
        one.start()

    lax.fori_loop(early, chunks, start_slabs, 0)
    for one in third_copies:
        one.wait_recv()

    total = gram_all[...].reshape(E, E + 128)
    eye = jnp.where(
        lax.broadcasted_iota(jnp.int32, (E, E), 0) == lax.broadcasted_iota(jnp.int32, (E, E), 1), 1.0, 0.0
    )
    shifts, weights = root_terms()
    for i, shift in enumerate(shifts):
        inv[i] = total[:, :E] * (1.0 / (E - 1.0)) + (1.0 + shift) * eye
    lane = lax.broadcasted_iota(jnp.int32, (1, E), 1)
    place = lax.broadcasted_iota(jnp.int32, (8, 1), 0)
    count = len(shifts)

    def sweep(n, _):
        at = pl.multiple_of(n * 8, 8)
        before = [inv[i, pl.ds(at, 8), :] for i in range(count)]
        panel = list(before)
        for k in range(8):
            here = lane == at + k
            for i in range(count):
                now = panel[i]
                col = jnp.sum(jnp.where(here, now, 0.0), axis=1, keepdims=True)
                pivot = 1.0 / col[k : k + 1]
                row = jnp.where(here, -pivot, now[k : k + 1] * pivot)
                panel[i] = jnp.where(place == k, row, jnp.where(here, 0.0, now) - col * row)
        inside = (lane >= at) & (lane < at + 8)
        for i in range(count):
            change = lax.dot_general(
                before[i], panel[i], (((0,), (0,)), ((), ())), precision=HIGH,
                preferred_element_type=jnp.float32,
            )
            inv[i] = jnp.where(inside, 0.0, inv[i]) - change
            inv[i, pl.ds(at, 8), :] = panel[i]
        return 0

    lax.fori_loop(0, E // 8, sweep, 0)
    root = 0.125 * eye
    for i, weight in enumerate(weights):
        root = root - weight * inv[i]
    inner = jnp.dot(root, total[:, E:], precision=HIGH, preferred_element_type=jnp.float32)
    extra = jnp.dot(root, inner, precision=HIGH, preferred_element_type=jnp.float32) * (1.0 / (E - 1.0))
    transform = root + extra[:, :1]
    transform = transform - jnp.sum(transform, axis=0, keepdims=True) * (1.0 / E) + 1.0 / E
    turned = transform.T

    lax.fori_loop(0, chunks, wait_slabs, 0)

    def back_copies(c):
        return [
            copy(mixed.at[peer("runner", k), c], back.at[c, pl.ds(2 + r * S, S)], back_s.at[k - 1, c],
                 back_r.at[k - 1, c], "runner", peer("runner", k))
            for k in range(1, R)
        ]

    for j in range(S):
        for f in range(fields):
            value = slab[:, :, j, f].reshape(E, C)
            result = jnp.dot(turned, value, precision=HIGH, preferred_element_type=jnp.float32)
            mixed[:, :, j, f] = result.reshape(R, chunks, mch, C)

    def give_back(c, _):
        for one in back_copies(c):
            one.start()
        back[c, pl.ds(2 + r * S, S)] = mixed[r, c]
        return 0

    lax.fori_loop(0, chunks, give_back, 0)

    def last_copies(c):
        return (
            copy(back.at[c, pl.ds(2, 2)], back.at[c, pl.ds(rows + 2, 2)], last_s.at[0, c], last_r.at[0, c],
                 "tile", down),
            copy(back.at[c, pl.ds(rows, 2)], back.at[c, pl.ds(0, 2)], last_s.at[1, c], last_r.at[1, c],
                 "tile", up),
        )

    def last_begin(c, _):
        for one in back_copies(c):
            one.wait_recv()
        for one in last_copies(c):
            one.start()
        return 0

    def last_end(c, _):
        for one in last_copies(c):
            one.wait_recv()

        def last_row(j, _):
            rates = tendency_row(lambda d, f: back[c, j + 2 + d, f])
            for f, rate in enumerate(rates):
                out[c, j, f] = back[c, j + 2, f] + TIME_STEP * rate
            return 0

        lax.fori_loop(0, rows, last_row, 0)
        return 0

    def last_both(c, _):
        last_begin(c, 0)
        last_end(c - 1, 0)
        return 0

    last_begin(0, 0)
    lax.fori_loop(1, chunks, last_both, 0)
    last_end(chunks - 1, 0)

    def drain(c, _):
        for s in range(4):
            for one in halos(s, c):
                one.wait_send()
        for one in (*slab_copies(c), *back_copies(c), *last_copies(c)):
            one.wait_send()
        return 0

    lax.fori_loop(0, chunks, drain, 0)
    for group in (cell_copies, pick_copies, first_copies, second_copies, third_copies):
        for one in group:
            one.wait_send()


def per_device(R, T, prior_mean_fields, ensemble_deviations, obs_cell, obs_value, obs_var):
    M, fields, rows, C = ensemble_deviations.shape
    E = M * R
    S = rows // R
    mch = 8
    chunks = M // mch
    obs = obs_cell.shape[-1]
    h = E // T
    start = prior_mean_fields[None] + ensemble_deviations
    start = start.reshape(chunks, mch, fields, rows, C).transpose(0, 3, 2, 1, 4)
    f32 = jnp.float32
    dma = pltpu.SemaphoreType.DMA
    vmem = pl.BlockSpec(memory_space=pltpu.VMEM)
    pairs = lambda n: [dma((n,)), dma((n,))]
    result = pl.pallas_call(
        functools.partial(kernel, R, T),
        out_shape=jax.ShapeDtypeStruct((chunks, rows, fields, mch, C), f32),
        in_specs=[vmem] * 4,
        out_specs=vmem,
        scratch_shapes=[
            pltpu.VMEM((4, chunks, rows + 4, fields, mch, C), f32),
            pltpu.VMEM((chunks, rows, fields, mch, C), f32),
            pltpu.VMEM((R, chunks, S, fields, mch, C), f32),
            pltpu.VMEM((R, 1, obs), jnp.int32),
            pltpu.VMEM((R, M, obs), f32),
            pltpu.VMEM((R, M, obs), f32),
            pltpu.VMEM((T, h, E + 128), f32),
            pltpu.VMEM((T, h, E + 128), f32),
            pltpu.VMEM((R, h, E + 128), f32),
            pltpu.VMEM((T, h, E + 128), f32),
            pltpu.VMEM((4, E, E), f32),
            pltpu.VMEM((R, chunks, S, fields, mch, C), f32),
            pltpu.VMEM((chunks, rows + 4, fields, mch, C), f32),
            dma((4, 2, chunks)), dma((4, 2, chunks)),
            *pairs(R - 1), *pairs(R - 1), *pairs(T - 1), *pairs(R - 1), *pairs(T - 1),
            dma((R - 1, chunks)), dma((R - 1, chunks)), dma((R - 1, chunks)), dma((R - 1, chunks)),
            dma((2, chunks)), dma((2, chunks)),
        ],
        compiler_params=pltpu.CompilerParams(
            collective_id=0, has_side_effects=True, vmem_limit_bytes=48 * 1024 * 1024
        ),
        name="forecast",
    )(start, obs_cell[0], obs_value[0], obs_var[0])
    return result.transpose(0, 3, 2, 1, 4).reshape(M, fields, rows, C)


def solution(mesh):
    placed = (
        P(None, "tile", None),
        P("runner", None, "tile", None),
        P("tile", "runner", None),
        P("tile", "runner", None),
        P("tile", "runner", None),
    )
    return jax.shard_map(
        functools.partial(per_device, mesh.shape["runner"], mesh.shape["tile"]),
        mesh=mesh,
        in_specs=placed,
        out_specs=P("runner", None, "tile", None),
        check_vma=False,
    )
```
